32 devices in a mesh: group: 2 (over x), mem: 16 (over z, y, core).
Axes of the slice: x: 2, y: 2, z: 4, core: 2. Of those that a mesh axis runs over, the one named last changes fastest.
Arguments:
- perturbations: bfloat16 [32, 256, 4, 1, 256], P(('group', 'mem')), parts along dimension 0, may hold values from -6 to 6
- gradient: bfloat16 [512, 4, 1, 256], P(('group', 'mem')), parts along dimension 0, may hold values from -6 to 6
Outputs:
- increment: bfloat16 [512, 4, 1, 256], P(('group', 'mem')), parts along dimension 0
The draws below stay inside these ranges and needn't reach their ends.
There are 2 independent parts, one for each index of `group`. The reference program is written for one: setup_inputs(seed, part) draws one part's arguments, and reference() takes and returns one part's arrays. A program takes and returns all parts, laid end to end along the dimension named above; each array names one. Nothing has to cross between parts.
All inputs are finite; a program needn't handle non-finite values.
Results may differ from the reference program's by a relative error of at most 0.0085.
Values may be sent and summed in bfloat16 or wider, within the bound.
A program may use at most 64 MiB of HBM per device.

```python
import jax
import jax.numpy as jnp
from jax import lax

NY = 256
NX = 256
NVAR = 4
LEV = 1
REACH = 8
MEMBERS = 16


def raised(array, key, source, target, shards_of, factor):
    def block_of(axis_at):
        return (jnp.arange(array.shape[axis_at]) // (array.shape[axis_at] // shards_of)).reshape((-1,) + (1,) * (array.ndim - 1 - axis_at))

    near = jax.random.permutation(key, shards_of)[block_of(target)]
    other_side = (block_of(target) + shards_of // 2) % shards_of
    return jnp.where((block_of(source) == near) | (block_of(source) == other_side), factor * array, array)


def levels(rng, extent, shards, smallest, high):
    gain = 1.0
    for position, shards_of in shards:
        steps = jax.random.uniform(jax.random.fold_in(jax.random.fold_in(rng, 6), position), (shards_of,), jnp.float32, smallest / len(shards), high / len(shards))
        gain = gain * jnp.repeat(jnp.exp(steps), extent[position] // shards_of).reshape((-1,) + (1,) * (len(extent) - 1 - position))
    return gain


def gaussian(stream_key, shape, spread, most, cuts=(), kind=jnp.bfloat16):
    gain = levels(stream_key, shape, cuts, -0.22, 0.18) if cuts else 1.0
    values = jax.random.normal(stream_key, shape, jnp.float32) * spread * gain
    return jnp.minimum(jnp.maximum(values, -most), most).astype(kind)


def bell_draw_with(key, shape, scale, most, split, heavy, kind=jnp.bfloat16):
    result = scale * jax.random.normal(key, shape, jnp.float32)
    if split:
        result = result * levels(key, shape, split, -0.22, 0.18)
    return jnp.clip(raised(result, jax.random.fold_in(key, 3), *heavy), -most, most).astype(kind)


def setup_inputs(seed: int = 0, part: int = 0) -> dict:
    key_list = jax.random.split(jax.random.key(seed), 3)
    own_keys = jax.random.split(jax.random.fold_in(key_list[2], part), 3)
    return {
        "perturbations": bell_draw_with(own_keys[0], (MEMBERS, NY, NVAR, LEV, NX), 1.0, 6.0, ((0, 16),), (0, 1, 16, 2.0)),
        "gradient": gaussian(own_keys[1], (NY, NVAR, LEV, NX), 1.0, 6.0, ((0, 16),)),
    }


def make_band(order):
    rows = jnp.arange(order, dtype=jnp.int32)
    offset = (rows[:, None] - rows[None, :]).astype(jnp.float32)
    weights = jnp.exp(-(offset * offset) / (4.0 * REACH))
    inside = jnp.abs(offset) <= REACH
    return jnp.where(inside, weights, jnp.float32(0.0)).astype(jnp.bfloat16)


def reference(perturbations, gradient):
    band_x = make_band(NX)
    band_y = make_band(NY)
    grad_wide = gradient.astype(jnp.float32)

    def one_member(total, member):
        mixed = jnp.sum(member.astype(jnp.float32) * grad_wide, axis=1).astype(jnp.bfloat16)
        along_x = jnp.dot(mixed.reshape(NY * LEV, NX), band_x, preferred_element_type=jnp.float32).astype(jnp.bfloat16)
        filtered = jnp.dot(band_y, along_x.reshape(NY, LEV * NX), preferred_element_type=jnp.float32).astype(jnp.bfloat16)
        filtered = filtered.reshape(NY, 1, LEV, NX).astype(jnp.float32)
        return total + member.astype(jnp.float32) * filtered, None

    start = jnp.zeros((NY, NVAR, LEV, NX), jnp.float32)
    total, unused = lax.scan(one_member, start, perturbations)
    return (total * (1.0 / (MEMBERS - 1))).astype(jnp.bfloat16)
```

```python
import functools

import jax
import jax.numpy as jnp
from jax import lax
from jax.experimental import pallas as pl
from jax.experimental.pallas import tpu as pltpu
from jax.sharding import PartitionSpec as P

REACH = 8
LANES = 128


def band_tile(order):
    rows = lax.broadcasted_iota(jnp.int32, (order, order), 0)
    cols = lax.broadcasted_iota(jnp.int32, (order, order), 1)
    offset = (rows - cols).astype(jnp.float32)
    weights = jnp.exp(-(offset * offset) / (4.0 * REACH))
    inside = jnp.abs(offset) <= REACH
    return jnp.where(inside, weights, jnp.float32(0.0)).astype(jnp.bfloat16)


def kernel(dims, pert_hbm, grad_ref, out_ref, pert, grads, prods, along, bandx, bandy, spread,
           own, pair_out, pair_in, row_out, row_in, far_out, far_in,
           load_sem, g1s, g1r, g2s, g2r, g3s, g3r, r1s, r1r, r2s, r2r, r3s, r3r):
    na, nb, nvars, tiles, local_rows = dims
    f32, bf16 = jnp.float32, jnp.bfloat16
    per = nvars * tiles
    size = local_rows * per
    group_rows = nb * 2 * local_rows
    me = lax.axis_index("mem")
    c = lax.rem(me, 2)
    b = lax.rem(me // 2, nb)
    a = me // (2 * nb)

    def at(a_, b_, c_):
        return (a_ * nb + b_) * 2 + c_

    def a_of(d):
        return lax.rem(a + d, na)

    def b_of(d):
        return lax.rem(b + d, nb)

    def remote(src, dst, send, recv, to):
        return pltpu.make_async_remote_copy(
            src_ref=src, dst_ref=dst, send_sem=send, recv_sem=recv,
            device_id={"mem": to}, device_id_type=pl.DeviceIdType.MESH)

    sibling = at(a, b, 1 - c)
    peers = [sibling] + [at(a_of(d), b, c) for d in range(1, na)] + [at(a, b_of(d), c) for d in range(1, nb)]
    load = pltpu.make_async_copy(pert_hbm, pert, load_sem)
    load.start()
    barrier = pltpu.get_barrier_semaphore()
    for peer in peers:
        pl.semaphore_signal(barrier, inc=1, device_id={"mem": peer}, device_id_type=pl.DeviceIdType.MESH)
    grads[me] = grad_ref[...]
    pl.semaphore_wait(barrier, len(peers))

    sends = []

    def send(copy):
        copy.start()
        sends.append(copy)

    def copy1(d):
        return remote(grads.at[me], grads.at[me], g1s.at[d], g1r.at[a], at(a_of(d), b, c))

    def copy2(da, db):
        block = grads.at[at(a_of(da), b, c)]
        return remote(block, block, g2s.at[da * nb + db], g2r.at[a_of(da) * nb + b], at(a, b_of(db), c))

    def copy3(da, db):
        j = a_of(da) * nb + b_of(db)
        block = grads.at[2 * j + c]
        return remote(block, block, g3s.at[j], g3r.at[j], sibling)

    a_order = sorted(range(1, na), key=lambda d: (-min(d, na - d), d))
    for d in a_order:
        send(copy1(d))
    for db in range(1, nb):
        send(copy2(0, db))
    send(copy3(0, 0))

    bandx[...] = band_tile(bandx.shape[0])
    bandy[...] = band_tile(bandy.shape[0])

    def multiply(j):
        rows = pl.ds(pl.multiple_of(j * size, size), size)
        prods[rows, :] = pert[rows, :].astype(f32) * grads[j].astype(f32)

    load.wait()
    multiply(me)
    nearest = sorted(range(1, na), key=lambda d: (min(d, na - d), d))
    for d in nearest:
        block = grads.at[at(a_of(d), b, c)]
        remote(block, block, g1s.at[0], g1r.at[a_of(d)], me).wait_recv()
        for db in range(1, nb):
            send(copy2(d, db))
        send(copy3(d, 0))
        multiply(at(a_of(d), b, c))
    for da in [0] + nearest:
        for db in range(1, nb):
            block = grads.at[at(a_of(da), b_of(db), c)]
            remote(block, block, g2s.at[0], g2r.at[a_of(da) * nb + b_of(db)], me).wait_recv()
            send(copy3(da, db))
            multiply(at(a_of(da), b_of(db), c))
        for db in range(nb):
            j = a_of(da) * nb + b_of(db)
            block = grads.at[2 * j + 1 - c]
            remote(block, block, g3s.at[0], g3r.at[j], me).wait_recv()
            multiply(2 * j + 1 - c)
        first = a_of(da) * group_rows
        halves = []
        for t in range(tiles):
            total = None
            for v in range(nvars):
                term = prods[pl.ds(first * per + t * nvars + v, group_rows, stride=per), :]
                total = term if total is None else total + term
            halves.append(total)
        mixed = jnp.concatenate(halves, axis=1).astype(bf16)
        rows = pl.ds(pl.multiple_of(first, group_rows), group_rows)
        along[rows, :] = jnp.dot(mixed, bandx[...], preferred_element_type=f32).astype(bf16)

    order = a_order + [0]

    def produce(d):
        group = a_of(d)
        rows = pl.ds(pl.multiple_of(group * group_rows, group_rows), group_rows)
        filtered = jnp.dot(bandy[rows, :], along[...], preferred_element_type=f32).astype(bf16).astype(f32)
        for t in range(tiles):
            for v in range(nvars):
                spread[pl.ds(t * nvars + v, group_rows, stride=per), :] = filtered[:, t * LANES:(t + 1) * LANES]

        def term(b_, c_):
            local = pl.ds(pl.multiple_of((b_ * 2 + c_) * size, size), size)
            whole = pl.ds(pl.multiple_of(at(group, b_, c_) * size, size), size)
            return spread[local, :] * pert[whole, :].astype(f32)

        for db in list(range(1, nb)) + [0]:
            j = group * nb + b_of(db)
            pair_out[j] = term(b_of(db), 1 - c).astype(bf16)
            send(remote(pair_out.at[j], pair_in.at[j], r1s.at[j], r1r.at[j], sibling))
        for db in range(nb):
            own[group * nb + b_of(db)] = term(b_of(db), c)

    def to_rows(d):
        group = a_of(d)
        for db in list(range(1, nb)) + [0]:
            j = group * nb + b_of(db)
            remote(pair_in.at[j], pair_in.at[j], r1s.at[0], r1r.at[j], me).wait_recv()
            total = own[j] + pair_in[j].astype(f32)
            if db == 0:
                own[j] = total
            else:
                row_out[j] = total.astype(bf16)
                send(remote(row_out.at[j], row_in.at[group * nb + b], r2s.at[j], r2r.at[group * nb + b],
                            at(a, b_of(db), c)))

    def to_far(d):
        group = a_of(d)
        total = own[group * nb + b]
        for db in range(1, nb):
            j = group * nb + b_of(db)
            remote(row_in.at[j], row_in.at[j], r2s.at[0], r2r.at[j], me).wait_recv()
            total = total + row_in[j].astype(f32)
        if d == 0:
            return total
        far_out[group] = total.astype(bf16)
        send(remote(far_out.at[group], far_in.at[a], r3s.at[group], r3r.at[a], at(group, b, c)))
        return None

    total = None
    for step in range(na + 2):
        if step < na:
            produce(order[step])
        if 0 <= step - 1 < na:
            to_rows(order[step - 1])
        if 0 <= step - 2 < na:
            total = to_far(order[step - 2])
    for d in nearest:
        j = a_of(d)
        remote(far_in.at[j], far_in.at[j], r3s.at[0], r3r.at[j], me).wait_recv()
        total = total + far_in[j].astype(f32)
    out_ref[...] = (total * (1.0 / (na * nb * 2 - 1))).astype(bf16)
    for copy in sends:
        copy.wait_send()


def flat(array):
    rows, nvars, columns = array.shape
    return array.reshape(rows, nvars, columns // LANES, LANES).transpose(0, 2, 1, 3).reshape(-1, LANES)


def per_device(perturbations, gradient):
    local_rows, nvars, levels, columns = gradient.shape
    grid_rows = perturbations.shape[1]
    count = lax.axis_size("mem")
    nb = 1
    while nb * nb * 4 <= count // 2:
        nb *= 2
    na = count // 2 // nb
    tiles = columns // LANES
    size = local_rows * nvars * tiles
    dma, bf16, f32 = pltpu.SemaphoreType.DMA, jnp.bfloat16, jnp.float32
    pairs = na * nb
    out = pl.pallas_call(
        functools.partial(kernel, (na, nb, nvars, tiles, local_rows)),
        out_shape=jax.ShapeDtypeStruct((size, LANES), bf16),
        in_specs=[pl.BlockSpec(memory_space=pl.ANY), pl.BlockSpec(memory_space=pltpu.VMEM)],
        out_specs=pl.BlockSpec(memory_space=pltpu.VMEM),
        scratch_shapes=[
            pltpu.VMEM((count * size, LANES), bf16),
            pltpu.VMEM((count, size, LANES), bf16),
            pltpu.VMEM((count * size, LANES), f32),
            pltpu.VMEM((grid_rows, columns), bf16),
            pltpu.VMEM((columns, columns), bf16),
            pltpu.VMEM((grid_rows, grid_rows), bf16),
            pltpu.VMEM((nb * 2 * size, LANES), f32),
            pltpu.VMEM((pairs, size, LANES), f32),
            pltpu.VMEM((pairs, size, LANES), bf16),
            pltpu.VMEM((pairs, size, LANES), bf16),
            pltpu.VMEM((pairs, size, LANES), bf16),
            pltpu.VMEM((pairs, size, LANES), bf16),
            pltpu.VMEM((na, size, LANES), bf16),
            pltpu.VMEM((na, size, LANES), bf16),
            dma,
            dma((na,)), dma((na,)),
            dma((pairs,)), dma((pairs,)),
            dma((pairs,)), dma((pairs,)),
            dma((pairs,)), dma((pairs,)),
            dma((pairs,)), dma((pairs,)),
            dma((na,)), dma((na,)),
        ],
        compiler_params=pltpu.CompilerParams(
            collective_id=0, has_side_effects=True, vmem_limit_bytes=60 * 2**20),
    )(flat(perturbations.reshape(grid_rows, nvars, columns)), flat(gradient.reshape(local_rows, nvars, columns)))
    out = out.reshape(local_rows, tiles, nvars, LANES).transpose(0, 2, 1, 3)
    return out.reshape(local_rows, nvars, levels, columns)


def solution(mesh):
    in_specs = (P(("group", "mem"), None, None, None, None), P(("group", "mem"), None, None, None))
    out_specs = P(("group", "mem"), None, None, None)
    return jax.shard_map(
        per_device, mesh=mesh, in_specs=in_specs, out_specs=out_specs, check_vma=False
    )
```

```python
import functools

import jax
import jax.numpy as jnp
from jax import lax
from jax.experimental import pallas as pl
from jax.experimental.pallas import tpu as pltpu
from jax.sharding import PartitionSpec as P

REACH = 8
LANES = 128


def band_tile(order):
    rows = lax.broadcasted_iota(jnp.int32, (order, order), 0)
    cols = lax.broadcasted_iota(jnp.int32, (order, order), 1)
    offset = (rows - cols).astype(jnp.float32)
    weights = jnp.exp(-(offset * offset) / (4.0 * REACH))
    inside = jnp.abs(offset) <= REACH
    return jnp.where(inside, weights, jnp.float32(0.0)).astype(jnp.bfloat16)


def kernel(dims, pert_hbm, grad_hbm, out_ref, pert, grads, prods, along, bandx, bandy, spread,
           own, pair_out, pair_in, far_out, far_in,
           load_sem, grad_sem, g1s, g1r, g2s, g2r, r1s, r1r, r2s, r2r):
    na, nb, nvars, tiles, local_rows = dims
    f32, bf16 = jnp.float32, jnp.bfloat16
    per = nvars * tiles
    size = local_rows * per
    group_rows = nb * 2 * local_rows
    me = lax.axis_index("mem")
    c = lax.rem(me, 2)
    b = lax.rem(me // 2, nb)
    a = me // (2 * nb)

    def at(a_, b_, c_):
        return (a_ * nb + b_) * 2 + c_

    def a_of(d):
        return lax.rem(a + d, na)

    def b_of(d):
        return lax.rem(b + d, nb)

    def remote(src, dst, send, recv, to):
        return pltpu.make_async_remote_copy(
            src_ref=src, dst_ref=dst, send_sem=send, recv_sem=recv,
            device_id={"mem": to}, device_id_type=pl.DeviceIdType.MESH)

    def arrived(ref, send, recv):
        remote(ref, ref, send, recv, sibling).wait_recv()

    sibling = at(a, b, 1 - c)
    near = sorted(range(na), key=lambda d: (min(d, na - d), d))
    far = near[::-1]
    chips = [(da, db) for da in far for db in list(range(1, nb)) + [0] if da or db]
    peers = [at(a_of(da), b_of(db), c) for da, db in chips] + [sibling]
    barrier = pltpu.get_barrier_semaphore()
    for peer in peers:
        pl.semaphore_signal(barrier, inc=1, device_id={"mem": peer}, device_id_type=pl.DeviceIdType.MESH)
    mine = grads.at[c, a, b]
    grad_load = pltpu.make_async_copy(grad_hbm, mine, grad_sem)
    grad_load.start()
    load = pltpu.make_async_copy(pert_hbm, pert, load_sem)
    load.start()
    grad_load.wait()
    pl.semaphore_wait(barrier, len(peers))

    sends = []

    def send(copy):
        copy.start()
        sends.append(copy)

    for da, db in chips:
        send(remote(mine, mine, g1s.at[da * nb + db], g1r.at[a * nb + b], at(a_of(da), b_of(db), c)))

    bandx[...] = band_tile(bandx.shape[0])
    bandy[...] = band_tile(bandy.shape[0])

    def multiply(a_, b_, c_):
        rows = pl.ds(pl.multiple_of(at(a_, b_, c_) * size, size), size)
        prods[rows, :] = pert[rows, :].astype(f32) * grads[c_, a_, b_].astype(f32)

    load.wait()
    for da in near:
        group = a_of(da)
        for db in range(nb):
            if da or db:
                arrived(grads.at[c, group, b_of(db)], g1s.at[0], g1r.at[group * nb + b_of(db)])
        block = grads.at[c, group]
        send(remote(block, block, g2s.at[group], g2r.at[group], sibling))
        for db in range(nb):
            multiply(group, b_of(db), c)
    for da in near:
        group = a_of(da)
        arrived(grads.at[1 - c, group], g2s.at[0], g2r.at[group])
        for db in range(nb):
            multiply(group, db, 1 - c)
        first = group * group_rows
        halves = []
        for t in range(tiles):
            total = None
            for v in range(nvars):
                term = prods[pl.ds(first * per + t * nvars + v, group_rows, stride=per), :]
                total = term if total is None else total + term
            halves.append(total)
        mixed = jnp.concatenate(halves, axis=1).astype(bf16)
        rows = pl.ds(pl.multiple_of(first, group_rows), group_rows)
        along[rows, :] = jnp.dot(mixed, bandx[...], preferred_element_type=f32).astype(bf16)

    def produce(d):
        group = a_of(d)
        rows = pl.ds(pl.multiple_of(group * group_rows, group_rows), group_rows)
        filtered = jnp.dot(bandy[rows, :], along[...], preferred_element_type=f32).astype(bf16).astype(f32)
        for t in range(tiles):
            for v in range(nvars):
                spread[pl.ds(t * nvars + v, group_rows, stride=per), :] = filtered[:, t * LANES:(t + 1) * LANES]

        def term(b_, c_):
            local = pl.ds(pl.multiple_of((b_ * 2 + c_) * size, size), size)
            whole = pl.ds(pl.multiple_of(at(group, b_, c_) * size, size), size)
            return spread[local, :] * pert[whole, :].astype(f32)

        for b_ in range(nb):
            pair_out[group, b_] = term(b_, 1 - c).astype(bf16)
        send(remote(pair_out.at[group], pair_in.at[group], r1s.at[group], r1r.at[group], sibling))
        for b_ in range(nb):
            own[group, b_] = term(b_, c)

    def forward(d):
        group = a_of(d)
        arrived(pair_in.at[group], r1s.at[0], r1r.at[group])
        for db in list(range(1, nb)) + [0]:
            b_ = b_of(db)
            total = own[group, b_] + pair_in[group, b_].astype(f32)
            if d == 0 and db == 0:
                return total
            j = group * nb + b_
            far_out[j] = total.astype(bf16)
            send(remote(far_out.at[j], far_in.at[a * nb + b], r2s.at[j], r2r.at[a * nb + b], at(group, b_, c)))
        return None

    total = None
    for step in range(na + 1):
        if step < na:
            produce(far[step])
        if step:
            total = forward(far[step - 1])
    for da, db in chips[::-1]:
        j = a_of(da) * nb + b_of(db)
        arrived(far_in.at[j], r2s.at[0], r2r.at[j])
        total = total + far_in[j].astype(f32)
    out_ref[...] = (total * (1.0 / (na * nb * 2 - 1))).astype(bf16)
    for copy in sends:
        copy.wait_send()


def flat(array):
    rows, nvars, columns = array.shape
    return array.reshape(rows, nvars, columns // LANES, LANES).transpose(0, 2, 1, 3).reshape(-1, LANES)


def per_device(perturbations, gradient):
    local_rows, nvars, levels, columns = gradient.shape
    grid_rows = perturbations.shape[1]
    count = lax.axis_size("mem")
    nb = 1
    while nb * nb * 4 <= count // 2:
        nb *= 2
    na = count // 2 // nb
    tiles = columns // LANES
    size = local_rows * nvars * tiles
    dma, bf16, f32 = pltpu.SemaphoreType.DMA, jnp.bfloat16, jnp.float32
    pairs = na * nb
    out = pl.pallas_call(
        functools.partial(kernel, (na, nb, nvars, tiles, local_rows)),
        out_shape=jax.ShapeDtypeStruct((size, LANES), bf16),
        in_specs=[pl.BlockSpec(memory_space=pltpu.HBM)] * 2,
        out_specs=pl.BlockSpec(memory_space=pltpu.VMEM),
        scratch_shapes=[
            pltpu.VMEM((count * size, LANES), bf16),
            pltpu.VMEM((2, na, nb, size, LANES), bf16),
            pltpu.VMEM((count * size, LANES), f32),
            pltpu.VMEM((grid_rows, columns), bf16),
            pltpu.VMEM((columns, columns), bf16),
            pltpu.VMEM((grid_rows, grid_rows), bf16),
            pltpu.VMEM((nb * 2 * size, LANES), f32),
            pltpu.VMEM((na, nb, size, LANES), f32),
            pltpu.VMEM((na, nb, size, LANES), bf16),
            pltpu.VMEM((na, nb, size, LANES), bf16),
            pltpu.VMEM((pairs, size, LANES), bf16),
            pltpu.VMEM((pairs, size, LANES), bf16),
            dma, dma,
            dma((pairs,)), dma((pairs,)),
            dma((na,)), dma((na,)),
            dma((na,)), dma((na,)),
            dma((pairs,)), dma((pairs,)),
        ],
        compiler_params=pltpu.CompilerParams(
            collective_id=0, has_side_effects=True, vmem_limit_bytes=60 * 2**20),
    )(flat(perturbations.reshape(grid_rows, nvars, columns)), flat(gradient.reshape(local_rows, nvars, columns)))
    out = out.reshape(local_rows, tiles, nvars, LANES).transpose(0, 2, 1, 3)
    return out.reshape(local_rows, nvars, levels, columns)


def solution(mesh):
    in_specs = (P(("group", "mem"), None, None, None, None), P(("group", "mem"), None, None, None))
    out_specs = P(("group", "mem"), None, None, None)
    return jax.shard_map(
        per_device, mesh=mesh, in_specs=in_specs, out_specs=out_specs, check_vma=False
    )
```

```python
import functools

import jax
import jax.numpy as jnp
from jax import lax
from jax.experimental import pallas as pl
from jax.experimental.pallas import tpu as pltpu
from jax.sharding import PartitionSpec as P

REACH = 8
LANES = 128


def band_tile(order):
    rows = lax.broadcasted_iota(jnp.int32, (order, order), 0)
    cols = lax.broadcasted_iota(jnp.int32, (order, order), 1)
    offset = (rows - cols).astype(jnp.float32)
    weights = jnp.exp(-(offset * offset) / (4.0 * REACH))
    inside = jnp.abs(offset) <= REACH
    return jnp.where(inside, weights, jnp.float32(0.0)).astype(jnp.bfloat16)


def kernel(dims, pert_hbm, grad_hbm, out_ref, pert, grads, prods, along, bandx, bandy, spread,
           own, pair_out, pair_in, far_out, far_in,
           load_sem, grad_sem, g1s, g1r, g2s, g2r, r1s, r1r, r2s, r2r):
    na, nb, nvars, tiles, local_rows = dims
    f32, bf16 = jnp.float32, jnp.bfloat16
    per = nvars * tiles
    size = local_rows * per
    group_rows = nb * 2 * local_rows
    me = lax.axis_index("mem")
    c = lax.rem(me, 2)
    b = lax.rem(me // 2, nb)
    a = me // (2 * nb)

    def at(a_, b_, c_):
        return (a_ * nb + b_) * 2 + c_

    def a_of(d):
        return lax.rem(a + d, na)

    def b_of(d):
        return lax.rem(b + d, nb)

    def remote(src, dst, send, recv, to):
        return pltpu.make_async_remote_copy(
            src_ref=src, dst_ref=dst, send_sem=send, recv_sem=recv,
            device_id={"mem": to}, device_id_type=pl.DeviceIdType.MESH)

    def arrived(ref, send, recv):
        remote(ref, ref, send, recv, sibling).wait_recv()

    sibling = at(a, b, 1 - c)
    near = sorted(range(na), key=lambda d: (min(d, na - d), d))
    far = near[::-1]
    chips = [(da, db) for da in far for db in list(range(1, nb)) + [0] if da or db]
    peers = [at(a_of(da), b_of(db), c) for da, db in chips] + [sibling]
    barrier = pltpu.get_barrier_semaphore()
    for peer in peers:
        pl.semaphore_signal(barrier, inc=1, device_id={"mem": peer}, device_id_type=pl.DeviceIdType.MESH)
    mine = grads.at[c, a, b]
    grad_load = pltpu.make_async_copy(grad_hbm, mine, grad_sem)
    grad_load.start()
    load = pltpu.make_async_copy(pert_hbm, pert, load_sem)
    load.start()
    grad_load.wait()
    pl.semaphore_wait(barrier, len(peers))

    sends = []

    def send(copy):
        copy.start()
        sends.append(copy)

    for da, db in chips:
        send(remote(mine, mine, g1s.at[da * nb + db], g1r.at[a * nb + b], at(a_of(da), b_of(db), c)))

    bandx[...] = band_tile(bandx.shape[0])
    bandy[...] = band_tile(bandy.shape[0])

    def multiply(a_, b_, c_):
        rows = pl.ds(pl.multiple_of(at(a_, b_, c_) * size, size), size)
        prods[rows, :] = pert[rows, :].astype(f32) * grads[c_, a_, b_].astype(f32)

    load.wait()
    for da in near:
        group = a_of(da)
        for db in range(nb):
            if da or db:
                arrived(grads.at[c, group, b_of(db)], g1s.at[0], g1r.at[group * nb + b_of(db)])
        block = grads.at[c, group]
        send(remote(block, block, g2s.at[group], g2r.at[group], sibling))
        for db in range(nb):
            multiply(group, b_of(db), c)
    for da in near:
        group = a_of(da)
        arrived(grads.at[1 - c, group], g2s.at[0], g2r.at[group])
        for db in range(nb):
            multiply(group, db, 1 - c)
        first = group * group_rows
        halves = []
        for t in range(tiles):
            total = None
            for v in range(nvars):
                term = prods[pl.ds(first * per + t * nvars + v, group_rows, stride=per), :]
                total = term if total is None else total + term
            halves.append(total)
        mixed = jnp.concatenate(halves, axis=1).astype(bf16)
        rows = pl.ds(pl.multiple_of(first, group_rows), group_rows)
        along[rows, :] = jnp.dot(mixed, bandx[...], preferred_element_type=f32).astype(bf16)

    def produce(d):
        group = a_of(d)
        rows = pl.ds(pl.multiple_of(group * group_rows, group_rows), group_rows)
        filtered = jnp.dot(bandy[rows, :], along[...], preferred_element_type=f32).astype(bf16).astype(f32)
        for t in range(tiles):
            for v in range(nvars):
                spread[pl.ds(t * nvars + v, group_rows, stride=per), :] = filtered[:, t * LANES:(t + 1) * LANES]

        def term(b_, c_):
            local = pl.ds(pl.multiple_of((b_ * 2 + c_) * size, size), size)
            whole = pl.ds(pl.multiple_of(at(group, b_, c_) * size, size), size)
            return spread[local, :] * pert[whole, :].astype(f32)

        for b_ in range(nb):
            pair_out[group, b_] = term(b_, 1 - c).astype(bf16)
        send(remote(pair_out.at[group], pair_in.at[group], r1s.at[group], r1r.at[group], sibling))
        for b_ in range(nb):
            own[group, b_] = term(b_, c)

    def forward(d):
        group = a_of(d)
        arrived(pair_in.at[group], r1s.at[0], r1r.at[group])
        for db in list(range(1, nb)) + [0]:
            b_ = b_of(db)
            total = own[group, b_] + pair_in[group, b_].astype(f32)
            if d == 0 and db == 0:
                return total
            j = group * nb + b_
            far_out[j] = total.astype(bf16)
            send(remote(far_out.at[j], far_in.at[a * nb + b], r2s.at[j], r2r.at[a * nb + b], at(group, b_, c)))
        return None

    total = None
    for step in range(na + 1):
        if step < na:
            produce(far[step])
        if step:
            total = forward(far[step - 1])
    for da, db in chips[::-1]:
        j = a_of(da) * nb + b_of(db)
        arrived(far_in.at[j], r2s.at[0], r2r.at[j])
        total = total + far_in[j].astype(f32)
    out_ref[...] = (total * (1.0 / (na * nb * 2 - 1))).astype(bf16)
    for copy in sends:
        copy.wait_send()


def flat(array):
    rows, nvars, columns = array.shape
    return array.reshape(rows, nvars, columns // LANES, LANES).transpose(0, 2, 1, 3).reshape(-1, LANES)


def per_device(perturbations, gradient):
    local_rows, nvars, levels, columns = gradient.shape
    grid_rows = perturbations.shape[1]
    count = lax.axis_size("mem")
    nb = 1
    while nb * nb * 4 <= count // 2:
        nb *= 2
    na = count // 2 // nb
    tiles = columns // LANES
    size = local_rows * nvars * tiles
    dma, bf16, f32 = pltpu.SemaphoreType.DMA, jnp.bfloat16, jnp.float32
    pairs = na * nb
    out = pl.pallas_call(
        functools.partial(kernel, (na, nb, nvars, tiles, local_rows)),
        out_shape=jax.ShapeDtypeStruct((size, LANES), bf16),
        in_specs=[pl.BlockSpec(memory_space=pltpu.HBM)] * 2,
        out_specs=pl.BlockSpec(memory_space=pltpu.VMEM),
        scratch_shapes=[
            pltpu.VMEM((count * size, LANES), bf16),
            pltpu.VMEM((2, na, nb, size, LANES), bf16),
            pltpu.VMEM((count * size, LANES), f32),
            pltpu.VMEM((grid_rows, columns), bf16),
            pltpu.VMEM((columns, columns), bf16),
            pltpu.VMEM((grid_rows, grid_rows), bf16),
            pltpu.VMEM((nb * 2 * size, LANES), f32),
            pltpu.VMEM((na, nb, size, LANES), f32),
            pltpu.VMEM((na, nb, size, LANES), bf16),
            pltpu.VMEM((na, nb, size, LANES), bf16),
            pltpu.VMEM((pairs, size, LANES), bf16),
            pltpu.VMEM((pairs, size, LANES), bf16),
            dma, dma,
            dma((pairs,)), dma((pairs,)),
            dma((na,)), dma((na,)),
            dma((na,)), dma((na,)),
            dma((pairs,)), dma((pairs,)),
        ],
        compiler_params=pltpu.CompilerParams(
            collective_id=0, has_side_effects=True, vmem_limit_bytes=56518246),
    )(flat(perturbations.reshape(grid_rows, nvars, columns)), flat(gradient.reshape(local_rows, nvars, columns)))
    out = out.reshape(local_rows, tiles, nvars, LANES).transpose(0, 2, 1, 3)
    return out.reshape(local_rows, nvars, levels, columns)


def solution(mesh):
    in_specs = (P(("group", "mem"), None, None, None, None), P(("group", "mem"), None, None, None))
    out_specs = P(("group", "mem"), None, None, None)
    return jax.shard_map(
        per_device, mesh=mesh, in_specs=in_specs, out_specs=out_specs, check_vma=False
    )
```
